1024 devices in a mesh: fsdp: 64 (over x, z), tensor: 16 (over y, core).
Axes of the slice: x: 4, y: 8, z: 16, core: 2. Of those that a mesh axis runs over, the one named last changes fastest.
Arguments:
- weights: bfloat16 [26624, 8192], P('fsdp', 'tensor'), may hold values from -3 to 3
- momentum: float32 [26624, 8192], P('fsdp', 'tensor'), may hold values from -540 to 540
- gradient: bfloat16 [26624, 8192], P('fsdp', 'tensor'), may hold values from -3 to 3
- right_factor: float32 [8192, 256], P('tensor'), may hold values from -0.0625 to 0.0625
Outputs:
- new_weights: bfloat16 [26624, 8192], P('fsdp', 'tensor')
- new_momentum: float32 [26624, 8192], P('fsdp', 'tensor')
- new_right: float32 [8192, 256], P('tensor')
The draws below stay inside these ranges and needn't reach their ends.
All inputs are finite; a program needn't handle non-finite values.
Results may differ from the reference program's by a relative error of at most 0.001.
Values sent between devices are 32-bit elements; how exact they have to be, the bound alone decides.
No kernel may reach another device: no remote copies, remote signals or barrier semaphores. Data moves between devices by JAX's collectives and lax.ppermute only.
A program may use at most 32 MiB of HBM per device.

```python
import math
import jax
import jax.numpy as jnp
from jax import lax

ROWS = 26624
COLS = 8192
RANK = 256


def draw_momentum(key, part):
    key = jax.random.fold_in(key, 11)
    key_base, key_rows, key_cols = jax.random.split(key, 3)
    row_ramp = 3.0 ** (jnp.arange(ROWS, dtype=jnp.float32) / ROWS)
    col_ramp = 3.0 ** (jnp.arange(COLS, dtype=jnp.float32) / COLS)
    base = jnp.clip(jax.random.normal(key_base, (ROWS, COLS), jnp.float32), -6.0, 6.0)
    span = math.log(10.0)
    row_scale = jnp.exp(jax.random.uniform(key_rows, (ROWS,), jnp.float32, 0.0, span)) * row_ramp
    col_scale = jnp.exp(jax.random.uniform(key_cols, (COLS,), jnp.float32, 0.0, span)) * col_ramp
    return 0.1 * base * row_scale[:, None] * col_scale[None, :]


def steps_of(rng, extent, cuts, smallest, high):
    def one(position, parts):
        heights = jax.random.uniform(jax.random.fold_in(jax.random.fold_in(rng, 6), position), (parts,), jnp.float32, smallest / len(cuts), high / len(cuts))
        return jnp.repeat(jnp.exp(heights), extent[position] // parts).reshape((-1,) + (1,) * (len(extent) - position - 1))

    level = one(*cuts[0])
    for cut in cuts[1:]:
        level = level * one(*cut)
    return level


def scatter_about(stream_key, dims, width, bound, cuts=(), kind=jnp.bfloat16):
    factor_of = steps_of(stream_key, dims, cuts, -0.22, 0.18) if cuts else 1.0
    values = jax.random.normal(stream_key, dims, jnp.float32) * width * factor_of
    return jnp.minimum(jnp.maximum(values, -bound), bound).astype(kind)


def setup_inputs(seed: int = 0) -> dict:
    seeds = jax.random.split(jax.random.key(seed), 5)
    weights = scatter_about(seeds[0], (ROWS, COLS), 0.5, 3.0, ((0, 64), (1, 16)))
    momentum = draw_momentum(jax.random.fold_in(seeds[4], 71), 0)
    gradient = scatter_about(seeds[2], (ROWS, COLS), 0.3, 3.0, ((0, 64), (1, 16)))
    right_factor = scatter_about(seeds[3], (COLS, RANK), COLS ** -0.5, 0.0625, ((0, 16),), jnp.float32)
    return {"weights": weights, "momentum": momentum, "gradient": gradient, "right_factor": right_factor}


def reference(weights, momentum, gradient, right_factor):
    high = lax.Precision.HIGHEST
    buffer = momentum + gradient.astype(jnp.float32)
    left = jnp.dot(buffer.astype(jnp.float32), right_factor.astype(jnp.float32), precision=high, preferred_element_type=jnp.float32)
    gram = jnp.dot(left.T.astype(jnp.float32), left.astype(jnp.float32), precision=high, preferred_element_type=jnp.float32)
    lower = jnp.linalg.cholesky(gram)
    basis = jax.scipy.linalg.solve_triangular(lower, left.T, lower=True).T
    right = jnp.dot(buffer.T.astype(jnp.float32), basis.astype(jnp.float32), precision=high, preferred_element_type=jnp.float32)
    norms_sq = lax.optimization_barrier(jnp.sum(right * right, axis=0))
    new_right = right / (jnp.sqrt(norms_sq) + 1e-06)
    new_momentum = buffer - 0.05 * jnp.dot(basis.astype(jnp.float32), right.T.astype(jnp.float32), precision=high, preferred_element_type=jnp.float32)
    factor = 0.2 * (ROWS * COLS / RANK) ** 0.5
    step_matrix = jnp.dot(basis.astype(jnp.float32), new_right.T.astype(jnp.float32), precision=high, preferred_element_type=jnp.float32)
    new_weights = (weights.astype(jnp.float32) - factor * step_matrix).astype(jnp.bfloat16)
    return (new_weights, new_momentum, new_right)
```

```python
import jax
import jax.numpy as jnp
from jax import lax
from jax.sharding import PartitionSpec as P

ROWS = 26624
COLS = 8192
RANK = 256
X = 4
Z = 16
T = 16
FACTOR = 0.2 * (ROWS * COLS / RANK) ** 0.5

GROUPS_X = [[x * Z + z for x in range(X)] for z in range(Z)]
GROUPS_Z = [[x * Z + z for z in range(Z)] for x in range(X)]


def dot(left_side, right_side, left_dim, right_dim, precision=lax.Precision.HIGHEST):
    return lax.dot_general(
        left_side,
        right_side,
        (((left_dim,), (right_dim,)), ((), ())),
        precision=precision,
        preferred_element_type=jnp.float32,
    )


def exchange(blocks, axis, groups=None):
    return lax.all_to_all(blocks, axis, 0, 0, axis_index_groups=groups)


def reduce_scatter(array, parts, axis, groups=None):
    blocks = array.reshape(parts, array.shape[0] // parts, array.shape[1])
    return jnp.sum(exchange(blocks, axis, groups), axis=0)


def gather(array, parts, axis, groups=None):
    blocks = exchange(jnp.broadcast_to(array, (parts, *array.shape)), axis, groups)
    return blocks.reshape(parts * array.shape[0], array.shape[1])


def inverse_factor(gram):
    lower = jnp.linalg.cholesky(gram)
    eye = jnp.eye(RANK, dtype=jnp.float32)
    return jax.scipy.linalg.solve_triangular(lower, eye, lower=True)


def on_device(weights, momentum, gradient, right_factor):
    buffer = momentum + gradient.astype(jnp.float32)
    part = dot(right_factor, buffer, 0, 1)
    left_t = lax.all_gather(reduce_scatter(part, T, "tensor"), "tensor", tiled=True)
    gram = dot(left_t, left_t, 1, 1)
    raw = dot(buffer, left_t, 0, 1)
    half = RANK // 2
    both = jnp.concatenate(
        [raw, jnp.concatenate([gram[:, :half], gram[:, half:]], axis=0)], axis=1
    )
    both = reduce_scatter(both, X, "fsdp", GROUPS_X)
    both = reduce_scatter(both, Z, "fsdp", GROUPS_Z)
    both = gather(both, Z, "fsdp", GROUPS_Z)
    both = gather(both, X, "fsdp", GROUPS_X)
    raw = both[:, :RANK]
    gram = jnp.concatenate([both[:RANK, RANK:], both[RANK:, RANK:]], axis=1)
    inverse = inverse_factor(gram)
    basis_t = dot(inverse, left_t, 1, 0)
    right = dot(raw, inverse, 1, 1)
    norms = jnp.sum(right * right, axis=0, keepdims=True)
    norms_sq = jnp.sum(exchange(jnp.broadcast_to(norms, (T, 1, RANK)), "tensor"), axis=0)
    new_right = right / (jnp.sqrt(norms_sq) + 1e-06)
    new_momentum = buffer - 0.05 * dot(basis_t, right, 0, 1)
    new_weights = (weights.astype(jnp.float32) - FACTOR * dot(basis_t, new_right, 0, 1)).astype(
        jnp.bfloat16
    )
    return (new_weights, new_momentum, new_right)


def solution(mesh):
    in_specs = (P("fsdp", "tensor"), P("fsdp", "tensor"), P("fsdp", "tensor"), P("tensor", None))
    out_specs = (P("fsdp", "tensor"), P("fsdp", "tensor"), P("tensor", None))
    return jax.shard_map(
        on_device, mesh=mesh, in_specs=in_specs, out_specs=out_specs, check_vma=False
    )
```

```python
import jax
import jax.numpy as jnp
from jax import lax
from jax.experimental import pallas as pl
from jax.experimental.pallas import tpu as pltpu
from jax.sharding import PartitionSpec as P

ROWS = 26624
COLS = 8192
RANK = 256
X = 4
Z = 16
T = 16
BLOCK = 64
HALF = RANK // 2
FACTOR = 0.2 * (ROWS * COLS / RANK) ** 0.5

GROUPS_X = [[x * Z + z for x in range(X)] for z in range(Z)]
GROUPS_Z = [[x * Z + z for z in range(Z)] for x in range(X)]


def dot(left_side, right_side, left_dim, right_dim, precision=lax.Precision.HIGHEST):
    return lax.dot_general(
        left_side,
        right_side,
        (((left_dim,), (right_dim,)), ((), ())),
        precision=precision,
        preferred_element_type=jnp.float32,
    )


def exchange(blocks, axis, groups=None):
    return lax.all_to_all(blocks, axis, 0, 0, axis_index_groups=groups)


def reduce_scatter(array, parts, axis, groups=None):
    blocks = array.reshape(parts, array.shape[0] // parts, array.shape[1])
    return jnp.sum(exchange(blocks, axis, groups), axis=0)


def gather(array, parts, axis, groups=None):
    blocks = exchange(jnp.broadcast_to(array, (parts, *array.shape)), axis, groups)
    return blocks.reshape(parts * array.shape[0], array.shape[1])


def lane(group, k):
    return jnp.broadcast_to(group[:, k : k + 1], group.shape)


def sublane(group, k):
    return jnp.broadcast_to(group[k : k + 1, :], group.shape)


def eliminate(groups):
    row = lax.broadcasted_iota(jnp.int32, groups[0].shape, 0)
    for p in range(len(groups)):
        rest = range(p, len(groups))
        column = {q: [lane(groups[q], 8 * p + k) for k in range(8)] for q in rest}
        pivots = jnp.ones_like(groups[p])
        for k in range(8):
            pivot = sublane(column[p][k], k)
            pivots = jnp.where(row == k, pivot, pivots)
            inverse = 1.0 / pivot
            pivot_row = sublane(groups[p], k)
            later = {j: sublane(column[p][j], k) for j in range(k + 1, 8)}
            for q in rest:
                ratio = column[q][k] * inverse
                if q == p:
                    ratio = jnp.where(row > k, ratio, 0.0)
                groups[q] = groups[q] - ratio * pivot_row
                for j in later:
                    column[q][j] = column[q][j] - ratio * later[j]
        groups[p] = groups[p] * lax.rsqrt(pivots)
    return groups


def factor_kernel(both_ref, inverse_ref, right_ref, norms_ref, work):
    work[:, :HALF] = both_ref[:RANK, RANK:]
    work[:, HALF:RANK] = both_ref[RANK:, RANK:]
    i = lax.broadcasted_iota(jnp.int32, (RANK, RANK), 0)
    j = lax.broadcasted_iota(jnp.int32, (RANK, RANK), 1)
    work[:, RANK:] = jnp.where(i == j, 1.0, 0.0)
    i = lax.broadcasted_iota(jnp.int32, (BLOCK, BLOCK), 0)
    j = lax.broadcasted_iota(jnp.int32, (BLOCK, BLOCK), 1)
    eye = jnp.where(i == j, 1.0, 0.0)
    for start in range(0, RANK, BLOCK):
        stop = start + BLOCK
        wide = jnp.concatenate([work[start:stop, :RANK][:, start:stop], eye], axis=1)
        groups = eliminate([wide[q : q + 8, :] for q in range(0, BLOCK, 8)])
        block = dot(jnp.concatenate(groups, axis=0)[:, BLOCK:], work[start:stop, :], 1, 0)
        inverse_ref[start:stop, :] = block[:, RANK:]
        if stop < RANK:
            work[stop:, :] = work[stop:, :] - dot(block[:, :RANK].T[stop:, :], block, 1, 0)
    right = dot(both_ref[:, :RANK], inverse_ref[...], 1, 1)
    right_ref[...] = right
    norms_ref[...] = jnp.sum(right * right, axis=0, keepdims=True)


def factor(both):
    cols = both.shape[0]
    return pl.pallas_call(
        factor_kernel,
        out_shape=(
            jax.ShapeDtypeStruct((RANK, RANK), jnp.float32),
            jax.ShapeDtypeStruct((cols, RANK), jnp.float32),
            jax.ShapeDtypeStruct((1, RANK), jnp.float32),
        ),
        in_specs=[pl.BlockSpec(memory_space=pltpu.VMEM)],
        out_specs=[pl.BlockSpec(memory_space=pltpu.VMEM)] * 3,
        scratch_shapes=[pltpu.VMEM((RANK, 2 * RANK), jnp.float32)],
        compiler_params=pltpu.CompilerParams(vmem_limit_bytes=24 * 2**20),
        cost_estimate=pl.CostEstimate(flops=10**9, bytes_accessed=2 * 10**6, transcendentals=0),
    )(both)


def on_device(weights, momentum, gradient, right_factor):
    buffer = momentum + gradient.astype(jnp.float32)
    part = dot(right_factor, buffer, 0, 1)
    left_t = lax.all_gather(reduce_scatter(part, T, "tensor"), "tensor", tiled=True)
    gram = dot(left_t, left_t, 1, 1)
    raw = dot(buffer, left_t, 0, 1)
    both = jnp.concatenate(
        [raw, jnp.concatenate([gram[:, :HALF], gram[:, HALF:]], axis=0)], axis=1
    )
    both = reduce_scatter(both, X, "fsdp", GROUPS_X)
    both = reduce_scatter(both, Z, "fsdp", GROUPS_Z)
    both = gather(both, Z, "fsdp", GROUPS_Z)
    both = gather(both, X, "fsdp", GROUPS_X)
    inverse, right, norms = factor(both)
    norms_sq = jnp.sum(exchange(jnp.broadcast_to(norms, (T, 1, RANK)), "tensor"), axis=0)
    basis_t = dot(inverse, left_t, 1, 0)
    new_right = right / (jnp.sqrt(norms_sq) + 1e-06)
    new_momentum = buffer - 0.05 * dot(basis_t, right, 0, 1, lax.Precision.HIGH)
    new_weights = (weights.astype(jnp.float32) - FACTOR * dot(basis_t, new_right, 0, 1, lax.Precision.HIGH)).astype(
        jnp.bfloat16
    )
    return (new_weights, new_momentum, new_right)


def solution(mesh):
    in_specs = (P("fsdp", "tensor"), P("fsdp", "tensor"), P("fsdp", "tensor"), P("tensor", None))
    out_specs = (P("fsdp", "tensor"), P("fsdp", "tensor"), P("tensor", None))
    return jax.shard_map(
        on_device, mesh=mesh, in_specs=in_specs, out_specs=out_specs, check_vma=False
    )
```

```python
import jax
import jax.numpy as jnp
from jax import lax
from jax.experimental import pallas as pl
from jax.experimental.pallas import tpu as pltpu
from jax.sharding import PartitionSpec as P

ROWS = 26624
COLS = 8192
RANK = 256
X = 4
Z = 16
T = 16
BLOCK = 64
HALF = RANK // 2
FACTOR = 0.2 * (ROWS * COLS / RANK) ** 0.5

ROW_Y = [[2 * y + core for y in range(T // 2)] for core in range(2)]
NEAR = [[x * Z + 2 * far + z for x in range(X) for z in range(2)] for far in range(Z // 2)]
FAR = [[x * Z + 2 * far + z for far in range(Z // 2)] for x in range(X) for z in range(2)]


def dot(left_side, right_side, left_dim, right_dim, precision=lax.Precision.HIGHEST):
    return lax.dot_general(
        left_side,
        right_side,
        (((left_dim,), (right_dim,)), ((), ())),
        precision=precision,
        preferred_element_type=jnp.float32,
    )


def exchange(blocks, axis, groups=None):
    return lax.all_to_all(blocks, axis, 0, 0, axis_index_groups=groups)


def reduce_scatter(array, parts, axis, groups=None):
    blocks = array.reshape(parts, array.shape[0] // parts, array.shape[1])
    return jnp.sum(exchange(blocks, axis, groups), axis=0)


def gather(array, parts, axis, groups=None):
    blocks = exchange(jnp.broadcast_to(array, (parts, *array.shape)), axis, groups)
    return blocks.reshape(parts * array.shape[0], array.shape[1])


def sum_over_tensor(part):
    core = lax.axis_index("tensor") % 2
    swap = [(t, t ^ 1) for t in range(T)]
    mine = lax.dynamic_slice_in_dim(part, core * HALF, HALF, 0)
    other = lax.dynamic_slice_in_dim(part, (1 - core) * HALF, HALF, 0)
    mine = mine + lax.ppermute(other, "tensor", swap)
    mine = gather(reduce_scatter(mine, T // 2, "tensor", ROW_Y), T // 2, "tensor", ROW_Y)
    other = lax.ppermute(mine, "tensor", swap)
    return jnp.where(
        core == 0, jnp.concatenate([mine, other], axis=0), jnp.concatenate([other, mine], axis=0)
    )


def lane(group, k):
    return jnp.broadcast_to(group[:, k : k + 1], group.shape)


def sublane(group, k):
    return jnp.broadcast_to(group[k : k + 1, :], group.shape)


def eliminate(groups):
    row = lax.broadcasted_iota(jnp.int32, groups[0].shape, 0)
    for p in range(len(groups)):
        rest = range(p, len(groups))
        column = {q: [lane(groups[q], 8 * p + k) for k in range(8)] for q in rest}
        pivots = jnp.ones_like(groups[p])
        for k in range(8):
            pivot = sublane(column[p][k], k)
            pivots = jnp.where(row == k, pivot, pivots)
            inverse = 1.0 / pivot
            pivot_row = sublane(groups[p], k)
            later = {j: sublane(column[p][j], k) for j in range(k + 1, 8)}
            for q in rest:
                ratio = column[q][k] * inverse
                if q == p:
                    ratio = jnp.where(row > k, ratio, 0.0)
                groups[q] = groups[q] - ratio * pivot_row
                for j in later:
                    column[q][j] = column[q][j] - ratio * later[j]
        groups[p] = groups[p] * lax.rsqrt(pivots)
    return groups


def factor_kernel(both_ref, inverse_ref, right_ref, norms_ref, work):
    work[:, :HALF] = both_ref[:RANK, RANK:]
    work[:, HALF:RANK] = both_ref[RANK:, RANK:]
    i = lax.broadcasted_iota(jnp.int32, (RANK, RANK), 0)
    j = lax.broadcasted_iota(jnp.int32, (RANK, RANK), 1)
    work[:, RANK:] = jnp.where(i == j, 1.0, 0.0)
    i = lax.broadcasted_iota(jnp.int32, (BLOCK, BLOCK), 0)
    j = lax.broadcasted_iota(jnp.int32, (BLOCK, BLOCK), 1)
    eye = jnp.where(i == j, 1.0, 0.0)
    for start in range(0, RANK, BLOCK):
        stop = start + BLOCK
        wide = jnp.concatenate([work[start:stop, :RANK][:, start:stop], eye], axis=1)
        groups = eliminate([wide[q : q + 8, :] for q in range(0, BLOCK, 8)])
        block = dot(jnp.concatenate(groups, axis=0)[:, BLOCK:], work[start:stop, :], 1, 0)
        inverse_ref[start:stop, :] = block[:, RANK:]
        if stop < RANK:
            work[stop:, :] = work[stop:, :] - dot(block[:, :RANK].T[stop:, :], block, 1, 0)
    right = dot(both_ref[:, :RANK], inverse_ref[...], 1, 1)
    right_ref[...] = right
    norms_ref[...] = jnp.sum(right * right, axis=0, keepdims=True)


def factor(both):
    cols = both.shape[0]
    return pl.pallas_call(
        factor_kernel,
        out_shape=(
            jax.ShapeDtypeStruct((RANK, RANK), jnp.float32),
            jax.ShapeDtypeStruct((cols, RANK), jnp.float32),
            jax.ShapeDtypeStruct((1, RANK), jnp.float32),
        ),
        in_specs=[pl.BlockSpec(memory_space=pltpu.VMEM)],
        out_specs=[pl.BlockSpec(memory_space=pltpu.VMEM)] * 3,
        scratch_shapes=[pltpu.VMEM((RANK, 2 * RANK), jnp.float32)],
        compiler_params=pltpu.CompilerParams(vmem_limit_bytes=24 * 2**20),
        cost_estimate=pl.CostEstimate(flops=10**9, bytes_accessed=2 * 10**6, transcendentals=0),
    )(both)


def on_device(weights, momentum, gradient, right_factor):
    buffer = momentum + gradient.astype(jnp.float32)
    part = dot(right_factor, buffer, 0, 1, lax.Precision.HIGH)
    left_t = sum_over_tensor(part)
    gram = dot(left_t, left_t, 1, 1)
    raw = dot(buffer, left_t, 0, 1, lax.Precision.HIGH)
    both = jnp.concatenate(
        [raw, jnp.concatenate([gram[:, :HALF], gram[:, HALF:]], axis=0)], axis=1
    )
    both = reduce_scatter(both, len(FAR), "fsdp", NEAR)
    both = reduce_scatter(both, len(NEAR), "fsdp", FAR)
    both = gather(both, len(NEAR), "fsdp", FAR)
    both = gather(both, len(FAR), "fsdp", NEAR)
    inverse, right, norms = factor(both)
    norms_sq = jnp.sum(exchange(jnp.broadcast_to(norms, (T, 1, RANK)), "tensor"), axis=0)
    basis_t = dot(inverse, left_t, 1, 0)
    new_right = right / (jnp.sqrt(norms_sq) + 1e-06)
    new_momentum = buffer - 0.05 * dot(basis_t, right, 0, 1, lax.Precision.HIGH)
    new_weights = (weights.astype(jnp.float32) - FACTOR * dot(basis_t, new_right, 0, 1, lax.Precision.HIGH)).astype(
        jnp.bfloat16
    )
    return (new_weights, new_momentum, new_right)


def solution(mesh):
    in_specs = (P("fsdp", "tensor"), P("fsdp", "tensor"), P("fsdp", "tensor"), P("tensor", None))
    out_specs = (P("fsdp", "tensor"), P("fsdp", "tensor"), P("tensor", None))
    return jax.shard_map(
        on_device, mesh=mesh, in_specs=in_specs, out_specs=out_specs, check_vma=False
    )
```

```python
import jax
import jax.numpy as jnp
from jax import lax
from jax.experimental import pallas as pl
from jax.experimental.pallas import tpu as pltpu
from jax.sharding import PartitionSpec as P

ROWS = 26624
COLS = 8192
RANK = 256
X = 4
Z = 16
T = 16
BLOCK = 128
HALF = RANK // 2
FACTOR = 0.2 * (ROWS * COLS / RANK) ** 0.5

ROW_Y = [[2 * y + core for y in range(T // 2)] for core in range(2)]
NEAR = [[x * Z + 2 * far + z for x in range(X) for z in range(2)] for far in range(Z // 2)]
FAR = [[x * Z + 2 * far + z for far in range(Z // 2)] for x in range(X) for z in range(2)]


def dot(left_side, right_side, left_dim, right_dim, precision=lax.Precision.HIGHEST):
    return lax.dot_general(
        left_side,
        right_side,
        (((left_dim,), (right_dim,)), ((), ())),
        precision=precision,
        preferred_element_type=jnp.float32,
    )


def dot3(left_side, right_side, left_dim, right_dim):
    left_high = left_side.astype(jnp.bfloat16)
    right_high = right_side.astype(jnp.bfloat16)
    left_low = (left_side - left_high.astype(jnp.float32)).astype(jnp.bfloat16)
    right_low = (right_side - right_high.astype(jnp.float32)).astype(jnp.bfloat16)
    dims = (left_dim, right_dim, lax.Precision.DEFAULT)
    small = dot(left_high, right_low, *dims) + dot(left_low, right_high, *dims)
    return small + dot(left_high, right_high, *dims)


def local_kernel(body, out_shape, *args, scalars=0, scratch=(), space=pltpu.VMEM, limit=24):
    places = [pl.BlockSpec(memory_space=pltpu.SMEM)] * scalars
    places += [pl.BlockSpec(memory_space=space)] * (len(args) - scalars)
    return pl.pallas_call(
        body,
        out_shape=[jax.ShapeDtypeStruct(shape, kind) for shape, kind in out_shape],
        in_specs=places,
        out_specs=[pl.BlockSpec(memory_space=pltpu.VMEM)] * len(out_shape),
        scratch_shapes=scratch,
        compiler_params=pltpu.CompilerParams(vmem_limit_bytes=limit * 2**20),
        cost_estimate=pl.CostEstimate(flops=10**9, bytes_accessed=2 * 10**6, transcendentals=0),
    )(*args)


def exchange(blocks, axis, groups=None):
    return lax.all_to_all(blocks, axis, 0, 0, axis_index_groups=groups)


def reduce_scatter(array, parts, axis, groups=None):
    blocks = array.reshape(parts, array.shape[0] // parts, array.shape[1])
    return jnp.sum(exchange(blocks, axis, groups), axis=0)


def gather(array, parts, axis, groups=None):
    blocks = exchange(jnp.broadcast_to(array, (parts, *array.shape)), axis, groups)
    return blocks.reshape(parts * array.shape[0], array.shape[1])


def sum_over_tensor(mine, other):
    swap = [(t, t ^ 1) for t in range(T)]
    mine = mine + lax.ppermute(other, "tensor", swap)
    mine = jnp.sum(exchange(mine, "tensor", ROW_Y), axis=0)
    mine = exchange(jnp.broadcast_to(mine, other.shape), "tensor", ROW_Y)
    return mine, lax.ppermute(mine, "tensor", swap)


def start_kernel(
    core, momentum, gradient, right_factor, mine, other, held, grad, factor, left, sems
):
    rows = momentum.shape[0]
    parts = [pl.ds(start, rows // 2) for start in (0, rows // 2)]
    first = pltpu.make_async_copy(right_factor, factor, sems.at[0])
    loads = [
        (
            pltpu.make_async_copy(momentum.at[part], held.at[part], sems.at[1 + 2 * i]),
            pltpu.make_async_copy(gradient.at[part], grad.at[part], sems.at[2 + 2 * i]),
        )
        for i, part in enumerate(parts)
    ]
    first.start()
    for load in loads:
        load[0].start()
        load[1].start()
    first.wait()
    for part, load in zip(parts, loads):
        load[0].wait()
        load[1].wait()
        total = held[part, :] + grad[part, :].astype(jnp.float32)
        left[part, :] = dot3(total, factor[...], 1, 0)
    step = rows // (T // 2)

    @pl.when(core[0] == 0)
    def _():
        for i in range(T // 2):
            mine[i] = left[step * i : step * (i + 1), :HALF]
            other[i] = left[step * i : step * (i + 1), HALF:]

    @pl.when(core[0] == 1)
    def _():
        for i in range(T // 2):
            mine[i] = left[step * i : step * (i + 1), HALF:]
            other[i] = left[step * i : step * (i + 1), :HALF]


def products_kernel(core, mine, other, momentum, gradient, left_t, both):
    mine_t = jnp.concatenate([mine[i] for i in range(T // 2)], axis=0).T
    other_t = jnp.concatenate([other[i] for i in range(T // 2)], axis=0).T

    @pl.when(core[0] == 0)
    def _():
        left_t[:HALF] = mine_t
        left_t[HALF:] = other_t

    @pl.when(core[0] == 1)
    def _():
        left_t[HALF:] = mine_t
        left_t[:HALF] = other_t

    buffer = momentum[...] + gradient[...].astype(jnp.float32)
    left = left_t[...]
    gram = dot(left, left, 1, 1)
    both[:RANK, RANK:] = gram[:, :HALF]
    both[RANK:, RANK:] = gram[:, HALF:]
    raw = dot3(left, buffer, 1, 0)
    both[:RANK, :RANK] = raw[:, :RANK]
    both[RANK:, :RANK] = raw[:, RANK:]


def momentum_kernel(inverse, left_t, right_t, momentum, gradient, basis, right, new_momentum):
    basis[...] = dot3(inverse[...], left_t[...], 1, 0).T
    right[...] = right_t[...].T
    buffer = momentum[...] + gradient[...].astype(jnp.float32)
    new_momentum[...] = buffer - 0.05 * dot3(basis[...], right_t[...], 1, 0)


def weights_kernel(norms, basis, right_t, right, weights, new_weights, new_right):
    scale = 1.0 / (jnp.sqrt(jnp.sum(norms[...], axis=0)) + 1e-06)
    new_right[...] = right[...] * scale
    step = dot3(basis[...] * (FACTOR * scale), right_t[...], 1, 0)
    new_weights[...] = (weights[...].astype(jnp.float32) - step).astype(jnp.bfloat16)


def lane(group, k):
    return jnp.broadcast_to(group[:, k : k + 1], group.shape)


def sublane(group, k):
    return jnp.broadcast_to(group[k : k + 1, :], group.shape)


def eliminate(groups):
    row = lax.broadcasted_iota(jnp.int32, groups[0].shape, 0)
    for p in range(len(groups)):
        rest = range(p, len(groups))
        column = {q: [lane(groups[q], 8 * p + k) for k in range(8)] for q in rest}
        pivots = jnp.ones_like(groups[p])
        for k in range(8):
            pivot = sublane(column[p][k], k)
            pivots = jnp.where(row == k, pivot, pivots)
            inverse = 1.0 / pivot
            pivot_row = sublane(groups[p], k)
            later = {j: sublane(column[p][j], k) for j in range(k + 1, 8)}
            for q in rest:
                ratio = column[q][k] * inverse
                if q == p:
                    ratio = jnp.where(row > k, ratio, 0.0)
                groups[q] = groups[q] - ratio * pivot_row
                for j in later:
                    column[q][j] = column[q][j] - ratio * later[j]
        groups[p] = groups[p] * lax.rsqrt(pivots)
    return groups


def factor_kernel(both_ref, inverse_ref, right_ref, norms_ref, work):
    work[:, :HALF] = both_ref[:RANK, RANK:]
    work[:, HALF:RANK] = both_ref[RANK:, RANK:]
    i = lax.broadcasted_iota(jnp.int32, (RANK, RANK), 0)
    j = lax.broadcasted_iota(jnp.int32, (RANK, RANK), 1)
    work[:, RANK:] = jnp.where(i == j, 1.0, 0.0)
    i = lax.broadcasted_iota(jnp.int32, (BLOCK, BLOCK), 0)
    j = lax.broadcasted_iota(jnp.int32, (BLOCK, BLOCK), 1)
    eye = jnp.where(i == j, 1.0, 0.0)
    for start in range(0, RANK, BLOCK):
        stop = start + BLOCK
        wide = jnp.concatenate([work[start:stop, :RANK][:, start:stop], eye], axis=1)
        groups = eliminate([wide[q : q + 8, :] for q in range(0, BLOCK, 8)])
        block = dot(jnp.concatenate(groups, axis=0)[:, BLOCK:], work[start:stop, :], 1, 0)
        inverse_ref[start:stop, :] = block[:, RANK:]
        if stop < RANK:
            work[stop:, :] = work[stop:, :] - dot(block[:, :RANK].T[stop:, :], block, 1, 0)
    inverse = inverse_ref[...]
    squares = jnp.zeros((RANK, HALF), jnp.float32)
    for half in range(2):
        right = dot3(inverse, both_ref[half * RANK : (half + 1) * RANK, :RANK], 1, 0)
        right_ref[:, half * RANK : (half + 1) * RANK] = right
        squares = squares + right[:, :HALF] * right[:, :HALF] + right[:, HALF:] * right[:, HALF:]
    norms = dot(jnp.ones((8, HALF), jnp.float32), squares, 1, 1)
    norms_ref[...] = jnp.broadcast_to(norms[:1].reshape(1, 1, RANK), norms_ref.shape)


def on_device(weights, momentum, gradient, right_factor):
    rows, cols = momentum.shape
    wide = jnp.float32
    blocks = (T // 2, rows // (T // 2), HALF)
    core = (lax.axis_index("tensor") % 2).reshape(1)
    mine, other = local_kernel(
        start_kernel,
        [(blocks, wide), (blocks, wide)],
        core, momentum, gradient, right_factor, scalars=1, space=pltpu.HBM, limit=56,
        scratch=[
            pltpu.VMEM((rows, cols), wide),
            pltpu.VMEM((rows, cols), jnp.bfloat16),
            pltpu.VMEM((cols, RANK), wide),
            pltpu.VMEM((rows, RANK), wide),
            pltpu.SemaphoreType.DMA((5,)),
        ],
    )
    mine, other = sum_over_tensor(mine, other)
    left_t, both = local_kernel(
        products_kernel,
        [((RANK, rows), wide), ((2 * RANK, RANK + HALF), wide)],
        core, mine, other, momentum, gradient, scalars=1,
    )
    both = reduce_scatter(both, len(FAR), "fsdp", NEAR)
    both = reduce_scatter(both, len(NEAR), "fsdp", FAR)
    both = gather(both, len(NEAR), "fsdp", FAR)
    both = gather(both, len(FAR), "fsdp", NEAR)
    inverse, right_t, norms = local_kernel(
        factor_kernel,
        [((RANK, RANK), wide), ((RANK, cols), wide), ((T, 1, RANK), wide)],
        both,
        scratch=[pltpu.VMEM((RANK, 2 * RANK), jnp.float32)],
    )
    norms = exchange(norms, "tensor")
    basis, right, new_momentum = local_kernel(
        momentum_kernel,
        [((rows, RANK), wide), ((cols, RANK), wide), ((rows, cols), wide)],
        inverse, left_t, right_t, momentum, gradient,
    )
    new_weights, new_right = local_kernel(
        weights_kernel,
        [((rows, cols), jnp.bfloat16), ((cols, RANK), wide)],
        norms, basis, right_t, right, weights,
    )
    return (new_weights, new_momentum, new_right)


def solution(mesh):
    in_specs = (P("fsdp", "tensor"), P("fsdp", "tensor"), P("fsdp", "tensor"), P("tensor", None))
    out_specs = (P("fsdp", "tensor"), P("fsdp", "tensor"), P("tensor", None))
    return jax.shard_map(
        on_device, mesh=mesh, in_specs=in_specs, out_specs=out_specs, check_vma=False
    )
```

```python
import jax
import jax.numpy as jnp
from jax import lax
from jax.experimental import pallas as pl
from jax.experimental.pallas import tpu as pltpu
from jax.sharding import PartitionSpec as P

ROWS = 26624
COLS = 8192
RANK = 256
X = 4
Z = 16
T = 16
BLOCK = 128
HALF = RANK // 2
FACTOR = 0.2 * (ROWS * COLS / RANK) ** 0.5

ROW_Y = [[2 * y + core for y in range(T // 2)] for core in range(2)]
NEAR = [[x * Z + 2 * far + z for x in range(X) for z in range(2)] for far in range(Z // 2)]
FAR = [[x * Z + 2 * far + z for far in range(Z // 2)] for x in range(X) for z in range(2)]


def dot(left_side, right_side, left_dim, right_dim, precision=lax.Precision.HIGHEST):
    return lax.dot_general(
        left_side,
        right_side,
        (((left_dim,), (right_dim,)), ((), ())),
        precision=precision,
        preferred_element_type=jnp.float32,
    )


def dot3(left_side, right_side, left_dim, right_dim):
    left_high = left_side.astype(jnp.bfloat16)
    right_high = right_side.astype(jnp.bfloat16)
    left_low = (left_side - left_high.astype(jnp.float32)).astype(jnp.bfloat16)
    right_low = (right_side - right_high.astype(jnp.float32)).astype(jnp.bfloat16)
    dims = (left_dim, right_dim, lax.Precision.DEFAULT)
    small = dot(left_high, right_low, *dims) + dot(left_low, right_high, *dims)
    return small + dot(left_high, right_high, *dims)


def local_kernel(body, out_shape, *args, scalars=0, scratch=(), space=pltpu.VMEM, limit=24):
    places = [pl.BlockSpec(memory_space=pltpu.SMEM)] * scalars
    places += [pl.BlockSpec(memory_space=space)] * (len(args) - scalars)
    return pl.pallas_call(
        body,
        out_shape=[jax.ShapeDtypeStruct(shape, kind) for shape, kind in out_shape],
        in_specs=places,
        out_specs=[pl.BlockSpec(memory_space=pltpu.VMEM)] * len(out_shape),
        scratch_shapes=scratch,
        compiler_params=pltpu.CompilerParams(vmem_limit_bytes=limit * 2**20),
        cost_estimate=pl.CostEstimate(flops=10**9, bytes_accessed=2 * 10**6, transcendentals=0),
    )(*args)


def exchange(blocks, axis, groups=None):
    return lax.all_to_all(blocks, axis, 0, 0, axis_index_groups=groups)


def reduce_scatter(array, parts, axis, groups=None):
    blocks = array.reshape(parts, array.shape[0] // parts, array.shape[1])
    return jnp.sum(exchange(blocks, axis, groups), axis=0)


def gather(array, parts, axis, groups=None):
    blocks = exchange(jnp.broadcast_to(array, (parts, *array.shape)), axis, groups)
    return blocks.reshape(parts * array.shape[0], array.shape[1])


def sum_over_tensor(mine, other):
    swap = [(t, t ^ 1) for t in range(T)]
    mine = mine + lax.ppermute(other, "tensor", swap)
    mine = jnp.sum(exchange(mine, "tensor", ROW_Y), axis=0)
    mine = exchange(jnp.broadcast_to(mine, other.shape), "tensor", ROW_Y)
    return mine, lax.ppermute(mine, "tensor", swap)


def start_kernel(
    core, momentum, gradient, right_factor, mine, other, held, grad, factor, left, sems
):
    rows = momentum.shape[0]
    parts = [pl.ds(start, rows // 2) for start in (0, rows // 2)]
    first = pltpu.make_async_copy(right_factor, factor, sems.at[0])
    loads = [
        (
            pltpu.make_async_copy(momentum.at[part], held.at[part], sems.at[1 + 2 * i]),
            pltpu.make_async_copy(gradient.at[part], grad.at[part], sems.at[2 + 2 * i]),
        )
        for i, part in enumerate(parts)
    ]
    first.start()
    for load in loads:
        load[0].start()
        load[1].start()
    first.wait()
    for part, load in zip(parts, loads):
        load[0].wait()
        load[1].wait()
        total = held[part, :] + grad[part, :].astype(jnp.float32)
        left[part, :] = dot3(total, factor[...], 1, 0)
    step = rows // (T // 2)

    @pl.when(core[0] == 0)
    def _():
        for i in range(T // 2):
            mine[i] = left[step * i : step * (i + 1), :HALF]
            other[i] = left[step * i : step * (i + 1), HALF:]

    @pl.when(core[0] == 1)
    def _():
        for i in range(T // 2):
            mine[i] = left[step * i : step * (i + 1), HALF:]
            other[i] = left[step * i : step * (i + 1), :HALF]


def products_kernel(core, mine, other, momentum, gradient, left_t, both):
    mine_t = jnp.concatenate([mine[i] for i in range(T // 2)], axis=0).T
    other_t = jnp.concatenate([other[i] for i in range(T // 2)], axis=0).T

    @pl.when(core[0] == 0)
    def _():
        left_t[:HALF] = mine_t
        left_t[HALF:] = other_t

    @pl.when(core[0] == 1)
    def _():
        left_t[HALF:] = mine_t
        left_t[:HALF] = other_t

    buffer = momentum[...] + gradient[...].astype(jnp.float32)
    left = left_t[...]
    gram = dot(left, left, 1, 1)
    both[:RANK, RANK:] = gram[:, :HALF]
    both[RANK:, RANK:] = gram[:, HALF:]
    raw = dot3(left, buffer, 1, 0)
    both[:RANK, :RANK] = raw[:, :RANK]
    both[RANK:, :RANK] = raw[:, RANK:]


def momentum_kernel(inverse, left_t, right_t, momentum, gradient, right, new_momentum):
    basis = dot3(inverse[...], left_t[...], 1, 0).T
    right[...] = right_t[...].T
    buffer = momentum[...] + gradient[...].astype(jnp.float32)
    new_momentum[...] = buffer - 0.05 * dot3(basis, right_t[...], 1, 0)


def weights_kernel(norms, inverse, left_t, right_t, right, weights, new_weights, new_right):
    scale = 1.0 / (jnp.sqrt(jnp.sum(norms[...], axis=0)) + 1e-06)
    new_right[...] = right[...] * scale
    basis = dot3(inverse[...], left_t[...], 1, 0).T
    step = dot3(basis * (FACTOR * scale), right_t[...], 1, 0)
    new_weights[...] = (weights[...].astype(jnp.float32) - step).astype(jnp.bfloat16)


def lane(group, k):
    return jnp.broadcast_to(group[:, k : k + 1], group.shape)


def sublane(group, k):
    return jnp.broadcast_to(group[k : k + 1, :], group.shape)


def eliminate(groups):
    row = lax.broadcasted_iota(jnp.int32, groups[0].shape, 0)
    for p in range(len(groups)):
        rest = range(p, len(groups))
        column = {q: [lane(groups[q], 8 * p + k) for k in range(8)] for q in rest}
        pivots = jnp.ones_like(groups[p])
        for k in range(8):
            pivot = sublane(column[p][k], k)
            pivots = jnp.where(row == k, pivot, pivots)
            inverse = 1.0 / pivot
            pivot_row = sublane(groups[p], k)
            later = {j: sublane(column[p][j], k) for j in range(k + 1, 8)}
            for q in rest:
                ratio = column[q][k] * inverse
                if q == p:
                    ratio = jnp.where(row > k, ratio, 0.0)
                groups[q] = groups[q] - ratio * pivot_row
                for j in later:
                    column[q][j] = column[q][j] - ratio * later[j]
        groups[p] = groups[p] * lax.rsqrt(pivots)
    return groups


def factor_kernel(both_ref, inverse_ref, right_ref, norms_ref, work):
    work[:, :HALF] = both_ref[:RANK, RANK:]
    work[:, HALF:RANK] = both_ref[RANK:, RANK:]
    i = lax.broadcasted_iota(jnp.int32, (RANK, RANK), 0)
    j = lax.broadcasted_iota(jnp.int32, (RANK, RANK), 1)
    work[:, RANK:] = jnp.where(i == j, 1.0, 0.0)
    i = lax.broadcasted_iota(jnp.int32, (BLOCK, BLOCK), 0)
    j = lax.broadcasted_iota(jnp.int32, (BLOCK, BLOCK), 1)
    eye = jnp.where(i == j, 1.0, 0.0)
    for start in range(0, RANK, BLOCK):
        stop = start + BLOCK
        wide = jnp.concatenate([work[start:stop, :RANK][:, start:stop], eye], axis=1)
        groups = eliminate([wide[q : q + 8, :] for q in range(0, BLOCK, 8)])
        block = dot(jnp.concatenate(groups, axis=0)[:, BLOCK:], work[start:stop, :], 1, 0)
        inverse_ref[start:stop, :] = block[:, RANK:]
        if stop < RANK:
            work[stop:, :] = work[stop:, :] - dot(block[:, :RANK].T[stop:, :], block, 1, 0)
    inverse = inverse_ref[...]
    squares = jnp.zeros((RANK, HALF), jnp.float32)
    for half in range(2):
        right = dot3(inverse, both_ref[half * RANK : (half + 1) * RANK, :RANK], 1, 0)
        right_ref[:, half * RANK : (half + 1) * RANK] = right
        squares = squares + right[:, :HALF] * right[:, :HALF] + right[:, HALF:] * right[:, HALF:]
    norms = dot(jnp.ones((8, HALF), jnp.float32), squares, 1, 1)
    norms_ref[...] = jnp.broadcast_to(norms[:1].reshape(1, 1, RANK), norms_ref.shape)


def on_device(weights, momentum, gradient, right_factor):
    rows, cols = momentum.shape
    wide = jnp.float32
    blocks = (T // 2, rows // (T // 2), HALF)
    core = (lax.axis_index("tensor") % 2).reshape(1)
    mine, other = local_kernel(
        start_kernel,
        [(blocks, wide), (blocks, wide)],
        core, momentum, gradient, right_factor, scalars=1, space=pltpu.HBM, limit=56,
        scratch=[
            pltpu.VMEM((rows, cols), wide),
            pltpu.VMEM((rows, cols), jnp.bfloat16),
            pltpu.VMEM((cols, RANK), wide),
            pltpu.VMEM((rows, RANK), wide),
            pltpu.SemaphoreType.DMA((5,)),
        ],
    )
    mine, other = sum_over_tensor(mine, other)
    left_t, both = local_kernel(
        products_kernel,
        [((RANK, rows), wide), ((2 * RANK, RANK + HALF), wide)],
        core, mine, other, momentum, gradient, scalars=1,
    )
    both = reduce_scatter(both, len(FAR), "fsdp", NEAR)
    both = reduce_scatter(both, len(NEAR), "fsdp", FAR)
    both = gather(both, len(NEAR), "fsdp", FAR)
    both = gather(both, len(FAR), "fsdp", NEAR)
    inverse, right_t, norms = local_kernel(
        factor_kernel,
        [((RANK, RANK), wide), ((RANK, cols), wide), ((T, 1, RANK), wide)],
        both,
        scratch=[pltpu.VMEM((RANK, 2 * RANK), jnp.float32)],
    )
    norms = exchange(norms, "tensor")
    right, new_momentum = local_kernel(
        momentum_kernel,
        [((cols, RANK), wide), ((rows, cols), wide)],
        inverse, left_t, right_t, momentum, gradient,
    )
    new_weights, new_right = local_kernel(
        weights_kernel,
        [((rows, cols), jnp.bfloat16), ((cols, RANK), wide)],
        norms, inverse, left_t, right_t, right, weights,
    )
    return (new_weights, new_momentum, new_right)


def solution(mesh):
    in_specs = (P("fsdp", "tensor"), P("fsdp", "tensor"), P("fsdp", "tensor"), P("tensor", None))
    out_specs = (P("fsdp", "tensor"), P("fsdp", "tensor"), P("tensor", None))
    return jax.shard_map(
        on_device, mesh=mesh, in_specs=in_specs, out_specs=out_specs, check_vma=False
    )
```
